256 devices in a mesh: ctx: 32 (over z, y), head: 8 (over x, core).
Axes of the slice: x: 4, y: 4, z: 8, core: 2. Of those that a mesh axis runs over, the one named last changes fastest.
Arguments:
- queries: bfloat16 [16384, 4096], P('ctx', 'head'), may hold values from -6 to 6
- keys: bfloat16 [16384, 8192], P('ctx', 'head'), may hold values from -6 to 6
- values: bfloat16 [16384, 8192], P('ctx', 'head'), may hold values from -6 to 6
- betas: float32 [16384, 64], P('ctx', 'head'), may hold values from 0 to 2
- initial_state: float32 [32, 128, 128], P('head'), may hold values from -48 to 48
- out_gain: float32 [4096], P('head'), may hold values from 0.1 to 1.9
Outputs:
- mixed: bfloat16 [16384, 4096], P(('ctx', 'head'))
The draws below stay inside these ranges and needn't reach their ends.
All inputs are finite; a program needn't handle non-finite values.
Results may differ from the reference program's by a relative error of at most 0.0033.
Values may be sent and summed in bfloat16 or wider, within the bound.
No kernel may reach another device: no remote copies, remote signals or barrier semaphores. Data moves between devices by JAX's collectives and lax.ppermute only.
A program may use at most 128 MiB of HBM per device.

```python
import jax
import jax.numpy as jnp
from jax import lax

ATTENTION_GROUPS = 32
DK = 128
DV = 128
GROUP = 64
TOK_DEV = 512
SEQUENCE_LENGTH = 16384


def draw_betas(key, part):
    key = jax.random.fold_in(key, 7)
    complete_lookup_vectors = jax.random.split(key, 6)
    slow_share = 0.5
    lagging_worker = jax.random.uniform(complete_lookup_vectors[0], (ATTENTION_GROUPS,), jnp.float32) < slow_share
    slow_device_delay = jnp.exp(jax.random.uniform(complete_lookup_vectors[1], (ATTENTION_GROUPS,), jnp.float32, jnp.log(0.05), jnp.log(0.5))) * DK / (2.0 * SEQUENCE_LENGTH)
    fast_gap = jax.random.uniform(complete_lookup_vectors[2], (ATTENTION_GROUPS,), jnp.float32, 0.3, 0.65)
    gap = jnp.where(lagging_worker, slow_device_delay, fast_gap)
    context_shards = SEQUENCE_LENGTH // TOK_DEV
    shard_scale = jax.random.uniform(complete_lookup_vectors[3], (context_shards, ATTENTION_GROUPS), jnp.float32, 1.0, 2.0)
    shard_scale = jnp.repeat(shard_scale, TOK_DEV, axis=0)
    rough = jax.random.uniform(complete_lookup_vectors[4], (SEQUENCE_LENGTH, ATTENTION_GROUPS, 2), jnp.float32, 0.5, 1.5)
    householder_beta = 2.0 - gap[None, :, None] * shard_scale[:, :, None] * rough
    position_span = jax.random.uniform(complete_lookup_vectors[5], (SEQUENCE_LENGTH, ATTENTION_GROUPS, 2), jnp.float32) < 1.0 / 512.0
    householder_beta = jnp.where(position_span & lagging_worker[None, :, None], 1.0, householder_beta)
    return householder_beta.reshape(SEQUENCE_LENGTH, 2 * ATTENTION_GROUPS).astype(jnp.float32)


def level_of(stream_key, extent, cuts, smallest, largest):
    def one(position, parts):
        heights = jax.random.uniform(jax.random.fold_in(jax.random.fold_in(stream_key, 6), position), (parts,), jnp.float32, smallest / len(cuts), largest / len(cuts))
        return jnp.repeat(jnp.exp(heights), extent[position] // parts).reshape((-1,) + (1,) * (len(extent) - position - 1))

    level = one(*cuts[0])
    for cut in cuts[1:]:
        level = level * one(*cut)
    return level


def scatter_about(own_key, shape, width, most, cuts=(), held_as=jnp.bfloat16):
    drawn = width * jax.random.normal(own_key, shape, jnp.float32)
    if cuts:
        drawn = drawn * level_of(own_key, shape, cuts, -0.22, 0.18)
    return jnp.clip(drawn, -most, most).astype(held_as)


def setup_inputs(seed: int = 0) -> dict:
    streams_of = jax.random.split(jax.random.key(seed), 7)
    queries = scatter_about(streams_of[0], (SEQUENCE_LENGTH, ATTENTION_GROUPS * DK), 1.0, 6.0, ((0, 32), (1, 8)))
    keys = scatter_about(streams_of[1], (SEQUENCE_LENGTH, 2 * ATTENTION_GROUPS * DK), 1.0, 6.0, ((0, 32), (1, 8)))
    values = scatter_about(streams_of[2], (SEQUENCE_LENGTH, 2 * ATTENTION_GROUPS * DV), 1.0, 6.0, ((0, 32), (1, 8)))
    betas = draw_betas(jax.random.fold_in(streams_of[6], 71), 0)
    initial_state = scatter_about(streams_of[4], (ATTENTION_GROUPS, DV, DK), 8.0, 48.0, ((0, 8),), jnp.float32)
    out_gain = jnp.clip(1.0 + 0.18 * jax.random.normal(streams_of[5], (ATTENTION_GROUPS * DV,), jnp.float32), 0.1, 1.9)
    return {"queries": queries, "keys": keys, "values": values, "betas": betas, "initial_state": initial_state, "out_gain": out_gain}


HIGH = lax.Precision.HIGHEST

def normalize(x):
    return x * lax.rsqrt(lax.optimization_barrier(jnp.sum(x * x, -1, keepdims=True)) + 1e-06)

def prepare(queries, keys, values, betas, heads):
    blocks = queries.shape[0] // GROUP
    qf = normalize(queries.astype(jnp.float32).reshape(blocks, GROUP, heads, DK))
    kf = normalize(keys.astype(jnp.float32).reshape(blocks, GROUP, heads, 2, DK))
    vf = values.astype(jnp.float32).reshape(blocks, GROUP, heads, 2, DV)
    bf = betas.reshape(blocks, GROUP, heads, 2)
    qc = qf.transpose(0, 2, 1, 3)
    kc = kf.transpose(0, 2, 1, 3, 4).reshape(blocks, heads, 2 * GROUP, DK)
    vc = vf.transpose(0, 2, 1, 3, 4).reshape(blocks, heads, 2 * GROUP, DV)
    bc = bf.transpose(0, 2, 1, 3).reshape(blocks, heads, 2 * GROUP)
    return (qc, kc, vc, bc)

def wy_factors(kc, vc, bc):
    items = kc.shape[-2]
    gram = jnp.einsum('...ik,...jk->...ij', kc, kc, precision=HIGH)
    system = jnp.tril(gram * bc[..., :, None], -1) + jnp.eye(items, dtype=jnp.float32)
    rhs = bc[..., :, None] * jnp.concatenate([kc, vc], -1)
    sol = lax.linalg.triangular_solve(system, rhs, left_side=True, lower=True, unit_diagonal=True)
    return (sol[..., :DK], sol[..., DK:])

def visible_mask():
    item_pos = jnp.arange(2 * GROUP, dtype=jnp.int32)[None, :]
    query_pos = jnp.arange(GROUP, dtype=jnp.int32)[:, None]
    return (item_pos <= 2 * query_pos + 1).astype(jnp.float32)

def reference(queries, keys, values, betas, initial_state, out_gain):
    blocks = SEQUENCE_LENGTH // GROUP
    visible = visible_mask()

    def step(state, index):
        start = (index * GROUP).astype(jnp.int32)
        qrows = lax.dynamic_slice_in_dim(queries, start, GROUP, 0)
        krows = lax.dynamic_slice_in_dim(keys, start, GROUP, 0)
        vrows = lax.dynamic_slice_in_dim(values, start, GROUP, 0)
        brows = lax.dynamic_slice_in_dim(betas, start, GROUP, 0)
        qc, kc, vc, bc = prepare(qrows, krows, vrows, brows, ATTENTION_GROUPS)
        qc, kc, vc, bc = (qc[0], kc[0], vc[0], bc[0])
        wmat, umat = wy_factors(kc, vc, bc)
        fresh = umat - jnp.einsum('hik,hvk->hiv', wmat, state, precision=HIGH)
        scores = jnp.einsum('hck,hik->hci', qc, kc, precision=HIGH) * visible
        result = jnp.einsum('hck,hvk->hcv', qc, state, precision=HIGH)
        result = result + jnp.einsum('hci,hiv->hcv', scores, fresh, precision=HIGH)
        state = state + jnp.einsum('hiv,hik->hvk', fresh, kc, precision=HIGH)
        return (state, result)
    final_state, outs = lax.scan(step, initial_state, jnp.arange(blocks, dtype=jnp.int32))
    scale = lax.rsqrt(lax.optimization_barrier(jnp.mean(outs * outs, -1, keepdims=True)) + 1e-06)
    mixed = outs * scale * out_gain.reshape(1, ATTENTION_GROUPS, 1, DV)
    return mixed.transpose(0, 2, 1, 3).reshape(SEQUENCE_LENGTH, ATTENTION_GROUPS * DV).astype(jnp.bfloat16)
```

```python
import functools
import jax
import jax.numpy as jnp
from jax import lax
from jax.experimental import pallas as pl
from jax.experimental.pallas import tpu as pltpu
from jax.sharding import PartitionSpec as P

D = 128
HALF = 64
ITEMS = 128
BLOCKS = 8
HEADS = 4
NY = 4
NZ = 8
F32 = jnp.float32
BF16 = jnp.bfloat16
VMEM_LIMIT = 48 * 1024 * 1024


def split(x):
    hi = x.astype(BF16)
    lo = (x - hi.astype(F32)).astype(BF16)
    return hi, lo


def mm(a, b):
    return lax.dot_general(a, b, (((1,), (0,)), ((), ())), preferred_element_type=F32)


def mm_nt(a, b):
    return lax.dot_general(a, b, (((1,), (1,)), ((), ())), preferred_element_type=F32)


def mm_tn(a, b):
    return lax.dot_general(a, b, (((0,), (0,)), ((), ())), preferred_element_type=F32)


def both(parts, axis):
    return jnp.concatenate(parts, axis)


def narrow3(ah, al, bh, bl):
    right = both([bh, bl], 1)
    out = mm(both([ah, al], 1), both([right, right], 0))
    return out[:, :D] + out[:, D:]


def wide3(ah, al, bh, bl):
    return mm(both([ah, al], 1), both([bh, bh], 0)) + mm(ah, bl)


def join(early, late):
    out = wide3(*split(late[:, :D]), *split(early))
    return both([out[:, :D], out[:, D:] + late[:, D:]], 1)


def order(shape, axis):
    place = lax.broadcasted_iota(jnp.int32, shape, axis)
    return 2 * (place % HALF) + place // HALF


def block_keys(ref, b):
    rows = slice(b * HALF, (b + 1) * HALF)
    return both([ref[rows, :D], ref[rows, D:]], 0)


def local_maps_kernel(k_ref, v_ref, b_ref, wu_ref, r_ref, tot_ref):
    shape = (ITEMS, ITEMS)
    ni, nj = order(shape, 0), order(shape, 1)
    eye = (ni == nj).astype(F32)
    masks = []
    for level in range(7):
        hit = ((ni >> (level + 1)) == (nj >> (level + 1))) & ((ni >> level) > (nj >> level))
        masks.append(hit.astype(F32))
    low = [m.astype(BF16) for m in masks]
    ks = [block_keys(k_ref, b) for b in range(BLOCKS)]
    grams = [mm_nt(k, k) for k in ks]
    squares = both([jnp.sum(g * eye, 0, keepdims=True) for g in grams], 0)
    rk = lax.rsqrt(squares + 1e-06)
    beta_rk = b_ref[0] * rk
    beta_rk2 = beta_rk * rk
    columns = beta_rk2.T
    lows = [columns[:, b : b + 1] * g for b, g in enumerate(grams)]
    inv = [eye - l * masks[0] for l in lows]
    pieces = [split(l) for l in lows]
    for level in range(1, 7):
        m = low[level]
        cut = [split(t) for t in inv]
        step = [narrow3(*t, p[0] * m, p[1] * m) for t, p in zip(cut, pieces)]
        inv = [t - narrow3(*split(x), *c) for t, x, c in zip(inv, step, cut)]
    maps = []
    for b in range(BLOCKS):
        v = block_keys(v_ref, b)
        w = mm(both(split(inv[b] * beta_rk2[b : b + 1]), 1), both([ks[b], ks[b]], 0))
        u = mm(both(split(inv[b] * beta_rk[b : b + 1]), 1), both([v, v], 0))
        wh, wl = split(w)
        uh, ul = split(u)
        wu = both([wh, uh, wl, ul], 1)
        wu_ref[0, b] = wu
        r = mm_tn(ks[b], wu)
        r = r[:, : 2 * D] + r[:, 2 * D :]
        maps.append(both([eye_minus(r[:, :D]), r[:, D:]], 1))
    total = maps[0]
    r_ref[0, 0] = jnp.zeros((D, 4 * D), BF16)
    for b in range(1, BLOCKS):
        th, tl = split(total)
        r_ref[0, b] = both([th, tl], 1)
        out = wide3(*split(maps[b][:, :D]), th, tl)
        total = both([out[:, :D], out[:, D:] + maps[b][:, D:]], 1)
    tot_ref[0] = total


def eye_minus(x):
    i = lax.broadcasted_iota(jnp.int32, x.shape, 0)
    j = lax.broadcasted_iota(jnp.int32, x.shape, 1)
    return (i == j).astype(F32) - x


def local_maps(keys, values, betas):
    return pl.pallas_call(
        local_maps_kernel,
        grid=(HEADS,),
        in_specs=[
            pl.BlockSpec((BLOCKS * HALF, 2 * D), lambda h: (0, h)),
            pl.BlockSpec((BLOCKS * HALF, 2 * D), lambda h: (0, h)),
            pl.BlockSpec((1, BLOCKS, ITEMS), lambda h: (h, 0, 0)),
        ],
        out_specs=[
            pl.BlockSpec((1, BLOCKS, ITEMS, 4 * D), lambda h: (h, 0, 0, 0)),
            pl.BlockSpec((1, BLOCKS, D, 4 * D), lambda h: (h, 0, 0, 0)),
            pl.BlockSpec((1, D, 2 * D), lambda h: (h, 0, 0)),
        ],
        out_shape=[
            jax.ShapeDtypeStruct((HEADS, BLOCKS, ITEMS, 4 * D), BF16),
            jax.ShapeDtypeStruct((HEADS, BLOCKS, D, 4 * D), BF16),
            jax.ShapeDtypeStruct((HEADS, D, 2 * D), F32),
        ],
        compiler_params=pltpu.CompilerParams(vmem_limit_bytes=VMEM_LIMIT),
        name="local_maps",
    )(keys, values, betas)


def outputs_kernel(q_ref, k_ref, wu_ref, r_ref, qe_ref, ol_ref):
    shape = (HALF, ITEMS)
    seen = (
        lax.broadcasted_iota(jnp.int32, shape, 1) % HALF <= lax.broadcasted_iota(jnp.int32, shape, 0)
    ).astype(F32)
    for b in range(BLOCKS):
        rows = slice(b * HALF, (b + 1) * HALF)
        q = q_ref[rows, :]
        qf = q.astype(F32)
        sh, sl = split(mm_nt(q, block_keys(k_ref, b)) * seen)
        wu = wu_ref[0, b]
        x = wide3(sh, sl, wu[:, : 2 * D], wu[:, 2 * D :])
        qe, ol = qf - x[:, :D], x[:, D:]
        if b:
            r = r_ref[0, b]
            e = wide3(*split(qe), r[:, : 2 * D], r[:, 2 * D :])
            qe, ol = e[:, :D], e[:, D:] + ol
        rq = lax.rsqrt(jnp.sum(qf * qf, -1, keepdims=True) + 1e-06)
        qe_ref[0, rows, :] = qe * rq
        ol_ref[0, rows, :] = ol * rq


def local_outputs(queries, keys, wu, prefixes):
    flops = 2 * HEADS * BLOCKS * HALF * D * D * 16
    return pl.pallas_call(
        outputs_kernel,
        grid=(HEADS,),
        in_specs=[
            pl.BlockSpec((BLOCKS * HALF, D), lambda h: (0, h)),
            pl.BlockSpec((BLOCKS * HALF, 2 * D), lambda h: (0, h)),
            pl.BlockSpec((1, BLOCKS, ITEMS, 4 * D), lambda h: (h, 0, 0, 0)),
            pl.BlockSpec((1, BLOCKS, D, 4 * D), lambda h: (h, 0, 0, 0)),
        ],
        out_specs=[
            pl.BlockSpec((1, BLOCKS * HALF, D), lambda h: (h, 0, 0)),
            pl.BlockSpec((1, BLOCKS * HALF, D), lambda h: (h, 0, 0)),
        ],
        out_shape=[jax.ShapeDtypeStruct((HEADS, BLOCKS * HALF, D), F32)] * 2,
        compiler_params=pltpu.CompilerParams(vmem_limit_bytes=VMEM_LIMIT),
        cost_estimate=pl.CostEstimate(flops=flops, bytes_accessed=12 * 1024 * 1024, transcendentals=0),
        name="local_outputs",
    )(queries, keys, wu, prefixes)


def in_vmem(n):
    return [pl.BlockSpec(memory_space=pltpu.VMEM)] * n


def in_smem():
    return [pl.BlockSpec(memory_space=pltpu.SMEM)]


def row_maps_kernel(me_ref, own_ref, r1, r2, r3, pre_ref, tot_ref, held):
    y = me_ref[0]
    held[y] = own_ref[y]
    for s, ref in ((1, r1), (2, r2), (3, r3)):
        held[(y + NY - s) % NY] = ref[...]
    total = held[0]
    for i in range(1, NY):
        pre_ref[i - 1] = total
        total = join(total, held[i])
    tot_ref[...] = total


def plane_maps_kernel(me_ref, own_ref, r1, r2, r3, s0_ref, pre_ref, end_ref, s0t_ref, held):
    y, z = me_ref[0], me_ref[1] % 4
    held[z] = own_ref[...]
    for s, ref in ((1, r1), (2, r2), (3, r3)):
        held[(z + 4 - s) % 4] = ref[...]
    start = s0_ref[y].T
    s0t_ref[...] = start
    total = held[0]
    pre_ref[...] = total
    for i in range(1, 4):
        @pl.when(z == i)
        def _():
            pre_ref[...] = total
        total = join(total, held[i])
    end_ref[...] = apply(total, start)


def apply(m, state):
    return narrow3(*split(m[:, :D]), *split(state)) + m[:, D:]


def states_kernel(me_ref, s0t_ref, mid_ref, pre_ref, rows_ref, out_ref):
    z = me_ref[1]
    late = (z >= 4).astype(F32)
    base = s0t_ref[...] * (1.0 - late) + mid_ref[...] * late
    inner = ((z % 4) > 0).astype(F32)
    moved = apply(pre_ref[...], base)
    state = moved * inner + base * (1.0 - inner)
    out_ref[0] = state
    for i in range(1, NY):
        out_ref[i] = apply(rows_ref[i - 1], state)


def finish_kernel(me_ref, s_own, s1, s2, s3, qe_ref, ol_ref, g_ref, out_ref):
    y = me_ref[0]
    for s in range(NY):
        h = (y + NY - s) % NY
        state = s_own[y] if s == 0 else (s1, s2, s3)[s - 1][...]
        raw = narrow3(*split(qe_ref[h]), *split(state)) + ol_ref[h]
        scale = lax.rsqrt(jnp.mean(raw * raw, -1, keepdims=True) + 1e-06)
        out_ref[:, pl.ds(pl.multiple_of(h * D, D), D)] = (raw * scale * g_ref[h]).astype(BF16)


def call(kernel, n_in, out_shape, scratch=(), name=None):
    return pl.pallas_call(
        kernel,
        in_specs=in_smem() + in_vmem(n_in),
        out_specs=jax.tree.map(lambda _: pl.BlockSpec(memory_space=pltpu.VMEM), out_shape),
        out_shape=out_shape,
        scratch_shapes=list(scratch),
        compiler_params=pltpu.CompilerParams(vmem_limit_bytes=VMEM_LIMIT),
        name=name,
    )


def shift_y(s):
    return [(z * NY + y, z * NY + (y + s) % NY) for z in range(NZ) for y in range(NY)]


def shift_z(s):
    return [
        (z * NY + y, (z // 4 * 4 + (z % 4 + s) % 4) * NY + y) for z in range(NZ) for y in range(NY)
    ]


ACROSS = [(z * NY + y, (z + 4) * NY + y) for z in range(4) for y in range(NY)]


def body(queries, keys, values, betas, initial_state, out_gain):
    f32 = lambda *shape: jax.ShapeDtypeStruct(shape, F32)
    place = lax.axis_index("ctx").astype(jnp.int32)
    y, z = place % NY, place // NY
    me = jnp.stack([y, z])
    bt = betas.reshape(BLOCKS, HALF, HEADS, 2).transpose(2, 0, 3, 1).reshape(HEADS, BLOCKS, ITEMS)
    wu, prefixes, total = local_maps(keys, values, bt)

    def exchange(array):
        return [
            lax.ppermute(lax.dynamic_index_in_dim(array, (y + s) % NY, 0, False), "ctx", shift_y(s))
            for s in (1, 2, 3)
        ]

    rows_pre, row_total = call(
        row_maps_kernel, 4, [f32(3, D, 2 * D), f32(D, 2 * D)], [pltpu.VMEM((4, D, 2 * D), F32)], "row_maps"
    )(me, total, *exchange(total))
    others = [lax.ppermute(row_total, "ctx", shift_z(s)) for s in (1, 2, 3)]
    plane_pre, end, start = call(
        plane_maps_kernel,
        5,
        [f32(D, 2 * D), f32(D, D), f32(D, D)],
        [pltpu.VMEM((4, D, 2 * D), F32)],
        "plane_maps",
    )(me, row_total, *others, initial_state)
    mid = lax.ppermute(end, "ctx", ACROSS)
    states = call(states_kernel, 4, f32(NY, D, D), (), "states")(me, start, mid, plane_pre, rows_pre)
    qe, ol = local_outputs(queries, keys, wu, prefixes)
    local_out = call(
        finish_kernel, 7, jax.ShapeDtypeStruct((BLOCKS * HALF, HEADS * D), BF16), (), "finish"
    )(me, states, *exchange(states), qe, ol, out_gain.reshape(HEADS, 1, D))
    return lax.all_to_all(local_out, "head", split_axis=0, concat_axis=1, tiled=True)


def solution(mesh):
    placed = (
        P("ctx", "head"),
        P("ctx", "head"),
        P("ctx", "head"),
        P("ctx", "head"),
        P("head", None, None),
        P("head"),
    )
    return jax.shard_map(
        body, mesh=mesh, in_specs=placed, out_specs=P(("ctx", "head"), None), check_vma=False
    )
```

```python
import functools
import jax
import jax.numpy as jnp
from jax import lax
from jax.experimental import pallas as pl
from jax.experimental.pallas import tpu as pltpu
from jax.sharding import PartitionSpec as P

D = 128
HALF = 64
ITEMS = 128
BLOCKS = 8
HEADS = 4
NY = 4
NZ = 8
F32 = jnp.float32
BF16 = jnp.bfloat16
VMEM_LIMIT = 48 * 1024 * 1024
OUTPUTS_LIMIT = 48 * 1024 * 1024
SMALL_LIMIT = 16 * 1024 * 1024
PER = 2


def split(x):
    hi = x.astype(BF16)
    lo = (x - hi.astype(F32)).astype(BF16)
    return hi, lo


def mm(a, b):
    return lax.dot_general(a, b, (((1,), (0,)), ((), ())), preferred_element_type=F32)


def mm_nt(a, b):
    return lax.dot_general(a, b, (((1,), (1,)), ((), ())), preferred_element_type=F32)


def mm_tn(a, b):
    return lax.dot_general(a, b, (((0,), (0,)), ((), ())), preferred_element_type=F32)


def both(parts, axis):
    return jnp.concatenate(parts, axis)


def narrow3(ah, al, bh, bl):
    right = both([bh, bl], 1)
    out = mm(both([ah, al], 1), both([right, right], 0))
    return out[:, :D] + out[:, D:]


def wide3(ah, al, bh, bl):
    return mm(both([ah, al], 1), both([bh, bh], 0)) + mm(ah, bl)


def join(early, late):
    out = wide3(*split(late[:, :D]), *split(early))
    return both([out[:, :D], out[:, D:] + late[:, D:]], 1)


def order(shape, axis):
    place = lax.broadcasted_iota(jnp.int32, shape, axis)
    return 2 * (place % HALF) + place // HALF


def block_keys(ref, h, b):
    rows = slice(b * HALF, (b + 1) * HALF)
    return both([ref[rows, 2 * h * D : (2 * h + 1) * D], ref[rows, (2 * h + 1) * D : (2 * h + 2) * D]], 0)


def stacked3(ah, al, bh, bl):
    rows = ah.shape[0]
    out = mm(both([ah, al], 0), both([bh, bl], 1))
    return out[:rows, :D] + out[:rows, D:] + out[rows:, :D]


def late_rows(x, width):
    return both([x[i : i + width] for i in range(width, ITEMS, 2 * width)], 0)


def drop_late(x, y, width):
    parts = []
    for n, i in enumerate(range(0, ITEMS, 2 * width)):
        parts += [x[i : i + width], x[i + width : i + 2 * width] - y[n * width : (n + 1) * width]]
    return both(parts, 0)


def item_betas(b_rows):
    left = lax.broadcasted_iota(jnp.int32, (1, ITEMS), 1) < HALF
    rows = []
    for h in range(PER):
        pair = [b_rows[pl.ds((pl.program_id(0) * PER + h) * 2 + j, 1), :] for j in range(2)]
        for c in range(BLOCKS // 2):
            lanes = slice(c * ITEMS, (c + 1) * ITEMS)
            first, second = pair[0][:, lanes], pair[1][:, lanes]
            rows.append(jnp.where(left, first, pltpu.roll(second, HALF, 1)))
            rows.append(jnp.where(left, pltpu.roll(first, HALF, 1), second))
    return both(rows, 0)


def local_maps_kernel(k_ref, v_ref, b_ref, wu_ref, r_ref, tot_ref):
    shape = (ITEMS, ITEMS)
    ni, nj = order(shape, 0), order(shape, 1)
    eye = (ni == nj).astype(F32)
    masks = []
    for level in range(7):
        hit = ((ni >> (level + 1)) == (nj >> (level + 1))) & ((ni >> level) > (nj >> level))
        masks.append(hit.astype(F32))
    low = [m.astype(BF16) for m in masks]
    units = [(h, b) for h in range(PER) for b in range(BLOCKS)]
    keys = [block_keys(k_ref, h, b) for h, b in units]
    grams = [mm_nt(k, k) for k in keys]
    squares = both([jnp.sum(g * eye, 0, keepdims=True) for g in grams], 0)
    pairs = both([jnp.sum(g * masks[0], 0, keepdims=True) for g in grams], 0)
    rk = lax.rsqrt(squares + 1e-06)
    beta_rk = item_betas(b_ref) * rk
    beta_rk2 = beta_rk * rk
    pairs = pairs * pltpu.roll(beta_rk2, HALF, 1)
    columns = beta_rk2.T
    pair_columns = pairs.T
    inv, pieces = [], []
    for i, g in enumerate(grams):
        l = columns[:, i : i + 1] * g
        x = l * masks[1]
        x = both([x[:HALF], x[HALF:] - pair_columns[:HALF, i : i + 1] * x[:HALF]], 0)
        x = x - pltpu.roll(x, HALF, 1) * pairs[i : i + 1]
        inv.append(eye - l * masks[0] - x)
        pieces.append(split(l))
    for level in range(2, 7):
        m = low[level]
        width = 1 << (level - 1)
        cut = [split(t) for t in inv]
        if width >= 8:
            left = [split(late_rows(t, width)) for t in inv] if width < 16 else [(late_rows(c[0], width), late_rows(c[1], width)) for c in cut]
        else:
            left = cut
        prod = stacked3 if width >= 8 else narrow3
        step = [prod(*t, p[0] * m, p[1] * m) for t, p in zip(left, pieces)]
        step = [prod(*split(x), *c) for x, c in zip(step, cut)]
        if width >= 8:
            inv = [drop_late(t, x, width) for t, x in zip(inv, step)]
        else:
            inv = [t - x for t, x in zip(inv, step)]
    maps = []
    for i, (h, b) in enumerate(units):
        v = block_keys(v_ref, h, b)
        w = mm(both(split(inv[i] * beta_rk2[i : i + 1]), 1), both([keys[i], keys[i]], 0))
        u = mm(both(split(inv[i] * beta_rk[i : i + 1]), 1), both([v, v], 0))
        wh, wl = split(w)
        uh, ul = split(u)
        wu = both([wh, uh, wl, ul], 1)
        wu_ref[h, b] = wu
        r = mm_tn(keys[i], wu)
        r = r[:, : 2 * D] + r[:, 2 * D :]
        maps.append(both([eye - r[:, :D], r[:, D:]], 1))

    def keep(h, b, m):
        hi, lo = split(m)
        r_ref[h, b - 1] = both([hi, lo], 1)

    two = [join(maps[i], maps[i + 1]) for i in range(0, len(maps), 2)]
    four = [join(two[i], two[i + 1]) for i in range(0, len(two), 2)]
    for h in range(PER):
        m, t, f = maps[h * 8 :], two[h * 4 :], four[h * 2 :]
        for b, node in ((1, m[0]), (2, t[0]), (3, m[2]), (4, f[0]), (5, m[4]), (6, t[2]), (7, m[6])):
            keep(h, b, node)
        tot_ref[h] = join(f[0], f[1])


def local_maps(keys, values, betas):
    return pl.pallas_call(
        local_maps_kernel,
        grid=(HEADS // PER,),
        in_specs=[
            pl.BlockSpec((BLOCKS * HALF, PER * 2 * D), lambda h: (0, h)),
            pl.BlockSpec((BLOCKS * HALF, PER * 2 * D), lambda h: (0, h)),
            pl.BlockSpec((2 * HEADS, BLOCKS * HALF), lambda h: (0, 0)),
        ],
        out_specs=[
            pl.BlockSpec((PER, BLOCKS, ITEMS, 4 * D), lambda h: (h, 0, 0, 0)),
            pl.BlockSpec((PER, BLOCKS - 1, D, 4 * D), lambda h: (h, 0, 0, 0)),
            pl.BlockSpec((PER, D, 2 * D), lambda h: (h, 0, 0)),
        ],
        out_shape=[
            jax.ShapeDtypeStruct((HEADS, BLOCKS, ITEMS, 4 * D), BF16),
            jax.ShapeDtypeStruct((HEADS, BLOCKS - 1, D, 4 * D), BF16),
            jax.ShapeDtypeStruct((HEADS, D, 2 * D), F32),
        ],
        compiler_params=pltpu.CompilerParams(vmem_limit_bytes=VMEM_LIMIT),
        name="local_maps",
    )(keys, values, betas)


def outputs_kernel(q_ref, k_ref, wu_ref, r_ref, qe_ref, ol_ref):
    shape = (HALF, ITEMS)
    seen = (
        lax.broadcasted_iota(jnp.int32, shape, 1) % HALF <= lax.broadcasted_iota(jnp.int32, shape, 0)
    ).astype(F32)
    node = [None] + [(r_ref[0, b][:, : 2 * D], r_ref[0, b][:, 2 * D :]) for b in range(BLOCKS - 1)]

    def onto(early, late):
        out = wide3(late[0][:, :D], late[1][:, :D], *early)
        added = late[0][:, D:].astype(F32) + late[1][:, D:].astype(F32)
        return split(both([out[:, :D], out[:, D:] + added], 1))

    prefix = list(node)
    prefix[3] = onto(node[2], node[3])
    prefix[5] = onto(node[4], node[5])
    prefix[6] = onto(node[4], node[6])
    prefix[7] = onto(prefix[6], node[7])
    for b in range(BLOCKS):
        rows = slice(b * HALF, (b + 1) * HALF)
        q = q_ref[rows, :]
        qf = q.astype(F32)
        sh, sl = split(mm_nt(q, block_keys(k_ref, 0, b)) * seen)
        wu = wu_ref[0, b]
        x = wide3(sh, sl, wu[:, : 2 * D], wu[:, 2 * D :])
        qe, ol = qf - x[:, :D], x[:, D:]
        if b:
            e = wide3(*split(qe), *prefix[b])
            qe, ol = e[:, :D], e[:, D:] + ol
        rq = lax.rsqrt(jnp.sum(qf * qf, -1, keepdims=True) + 1e-06)
        qe_ref[0, rows, :] = qe * rq
        ol_ref[0, rows, :] = ol * rq


def local_outputs(queries, keys, wu, prefixes):
    flops = 2 * HEADS * BLOCKS * HALF * D * D * 16
    return pl.pallas_call(
        outputs_kernel,
        grid=(HEADS,),
        in_specs=[
            pl.BlockSpec((BLOCKS * HALF, D), lambda h: (0, h)),
            pl.BlockSpec((BLOCKS * HALF, 2 * D), lambda h: (0, h)),
            pl.BlockSpec((1, BLOCKS, ITEMS, 4 * D), lambda h: (h, 0, 0, 0)),
            pl.BlockSpec((1, BLOCKS - 1, D, 4 * D), lambda h: (h, 0, 0, 0)),
        ],
        out_specs=[
            pl.BlockSpec((1, BLOCKS * HALF, D), lambda h: (h, 0, 0)),
            pl.BlockSpec((1, BLOCKS * HALF, D), lambda h: (h, 0, 0)),
        ],
        out_shape=[jax.ShapeDtypeStruct((HEADS, BLOCKS * HALF, D), F32)] * 2,
        compiler_params=pltpu.CompilerParams(vmem_limit_bytes=OUTPUTS_LIMIT),
        cost_estimate=pl.CostEstimate(flops=flops, bytes_accessed=12 * 1024 * 1024, transcendentals=0),
        name="local_outputs",
    )(queries, keys, wu, prefixes)


def in_vmem(n):
    return [pl.BlockSpec(memory_space=pltpu.VMEM)] * n


def in_smem():
    return [pl.BlockSpec(memory_space=pltpu.SMEM)]


def row_maps_kernel(me_ref, own_ref, r1, r2, r3, pre_ref, tot_ref, held):
    y = me_ref[0]
    held[y] = own_ref[...]
    for s, ref in ((1, r1), (2, r2), (3, r3)):
        held[(y + NY - s) % NY] = ref[...]
    two = join(held[0], held[1])
    pre_ref[0] = held[0]
    pre_ref[1] = two
    pre_ref[2] = join(two, held[2])
    tot_ref[...] = join(two, join(held[2], held[3]))


def plane_maps_kernel(me_ref, own_ref, r1, r2, r3, s0_ref, pre_ref, end_ref, s0t_ref, held):
    y, z = me_ref[0], me_ref[1] % 4
    held[z] = own_ref[...]
    for s, ref in ((1, r1), (2, r2), (3, r3)):
        held[(z + 4 - s) % 4] = ref[...]
    start = s0_ref[y].T
    s0t_ref[...] = start
    two = join(held[0], held[1])
    prefixes = (held[0], two, join(two, held[2]))
    pre_ref[...] = prefixes[0]
    for i in (2, 3):

        @pl.when(z == i)
        def _():
            pre_ref[...] = prefixes[i - 1]

    end_ref[...] = apply(join(held[2], held[3]), apply(two, start))


def apply(m, state):
    return narrow3(*split(m[:, :D]), *split(state)) + m[:, D:]


def states_kernel(me_ref, s0t_ref, mid_ref, pre_ref, rows_ref, out_ref):
    z = me_ref[1]
    base = jnp.where(z >= 4, mid_ref[...], s0t_ref[...])
    state = jnp.where(z % 4 > 0, apply(pre_ref[...], base), base)
    out_ref[0] = state
    for i in range(1, NY):
        out_ref[i] = apply(rows_ref[i - 1], state)


def finish_kernel(me_ref, s_own, s1, s2, s3, qe_ref, ol_ref, g_ref, out_ref):
    y = me_ref[0]
    for s in range(NY):
        h = (y + NY - s) % NY
        state = (s_own, s1, s2, s3)[s][...]
        raw = narrow3(*split(qe_ref[h]), *split(state)) + ol_ref[h]
        scale = lax.rsqrt(jnp.mean(raw * raw, -1, keepdims=True) + 1e-06)
        out_ref[:, pl.ds(pl.multiple_of(h * D, D), D)] = (raw * scale * g_ref[h]).astype(BF16)


def call(kernel, n_in, out_shape, scratch=(), name=None):
    return pl.pallas_call(
        kernel,
        in_specs=in_smem() + in_vmem(n_in),
        out_specs=jax.tree.map(lambda _: pl.BlockSpec(memory_space=pltpu.VMEM), out_shape),
        out_shape=out_shape,
        scratch_shapes=list(scratch),
        compiler_params=pltpu.CompilerParams(vmem_limit_bytes=SMALL_LIMIT),
        name=name,
    )


def shift_y(s):
    return [(z * NY + y, z * NY + (y + s) % NY) for z in range(NZ) for y in range(NY)]


def shift_z(s):
    return [
        (z * NY + y, (z // 4 * 4 + (z % 4 + s) % 4) * NY + y) for z in range(NZ) for y in range(NY)
    ]


ACROSS = [(a * NY + y, b * NY + y) for a, b in zip(range(NZ), (7, 6, 5, 4, 3, 2, 1, 0)) for y in range(NY)]


def body(queries, keys, values, betas, initial_state, out_gain):
    f32 = lambda *shape: jax.ShapeDtypeStruct(shape, F32)
    place = lax.axis_index("ctx").astype(jnp.int32)
    y, z = place % NY, place // NY
    me = jnp.stack([y, z])
    wu, prefixes, total = local_maps(keys, values, betas.T)

    def exchange(array):
        mine = [lax.dynamic_index_in_dim(array, (y + s) % NY, 0, False) for s in range(NY)]
        return mine[:1] + [lax.ppermute(mine[s], "ctx", shift_y(s)) for s in (1, 2, 3)]

    rows_pre, row_total = call(
        row_maps_kernel, 4, [f32(3, D, 2 * D), f32(D, 2 * D)], [pltpu.VMEM((4, D, 2 * D), F32)], "row_maps"
    )(me, *exchange(total))
    others = [lax.ppermute(row_total, "ctx", shift_z(s)) for s in (1, 2, 3)]
    qe, ol = local_outputs(queries, keys, wu, prefixes)
    others, qe, ol = lax.optimization_barrier((others, qe, ol))
    plane_pre, end, start = call(
        plane_maps_kernel,
        5,
        [f32(D, 2 * D), f32(D, D), f32(D, D)],
        [pltpu.VMEM((4, D, 2 * D), F32)],
        "plane_maps",
    )(me, row_total, *others, initial_state)
    mid = lax.ppermute(end, "ctx", ACROSS)
    states = call(states_kernel, 4, f32(NY, D, D), (), "states")(me, start, mid, plane_pre, rows_pre)
    local_out = call(
        finish_kernel, 7, jax.ShapeDtypeStruct((BLOCKS * HALF, HEADS * D), BF16), (), "finish"
    )(me, *exchange(states), qe, ol, out_gain.reshape(HEADS, 1, D))
    return lax.all_to_all(local_out, "head", split_axis=0, concat_axis=1, tiled=True)


def solution(mesh):
    placed = (
        P("ctx", "head"),
        P("ctx", "head"),
        P("ctx", "head"),
        P("ctx", "head"),
        P("head", None, None),
        P("head"),
    )
    return jax.shard_map(
        body, mesh=mesh, in_specs=placed, out_specs=P(("ctx", "head"), None), check_vma=False
    )
```

```python
import functools
import jax
import jax.numpy as jnp
from jax import lax
from jax.experimental import pallas as pl
from jax.experimental.pallas import tpu as pltpu
from jax.sharding import PartitionSpec as P

D = 128
HALF = 64
ITEMS = 128
BLOCKS = 8
HEADS = 4
NY = 4
EARLY = 2
NZ = 8
F32 = jnp.float32
BF16 = jnp.bfloat16
VMEM_LIMIT = 53 * 1024 * 1024
TERMS_LIMIT = 60 * 1024 * 1024
OUTPUTS_LIMIT = 48 * 1024 * 1024
SMALL_LIMIT = 16 * 1024 * 1024
PER = 2


def split(x):
    hi = x.astype(BF16)
    lo = (x - hi.astype(F32)).astype(BF16)
    return hi, lo


def mm(a, b):
    return lax.dot_general(a, b, (((1,), (0,)), ((), ())), preferred_element_type=F32)


def mm_nt(a, b):
    return lax.dot_general(a, b, (((1,), (1,)), ((), ())), preferred_element_type=F32)


def mm_tn(a, b):
    return lax.dot_general(a, b, (((0,), (0,)), ((), ())), preferred_element_type=F32)


def both(parts, axis):
    return jnp.concatenate(parts, axis)


def narrow3(ah, al, bh, bl):
    right = both([bh, bl], 1)
    out = mm(both([ah, al], 1), both([right, right], 0))
    return out[:, :D] + out[:, D:]


def wide3(ah, al, bh, bl):
    return mm(both([ah, al], 1), both([bh, bh], 0)) + mm(ah, bl)


def join(early, late):
    out = wide3(*split(late[:, :D]), *split(early))
    return both([out[:, :D], out[:, D:] + late[:, D:]], 1)


def order(shape, axis):
    place = lax.broadcasted_iota(jnp.int32, shape, axis)
    return 2 * (place % HALF) + place // HALF


def block_keys(ref, h, b):
    rows = slice(b * HALF, (b + 1) * HALF)
    return both([ref[rows, 2 * h * D : (2 * h + 1) * D], ref[rows, (2 * h + 1) * D : (2 * h + 2) * D]], 0)


def stacked3(ah, al, bh, bl):
    rows = ah.shape[0]
    out = mm(both([ah, al], 0), both([bh, bl], 1))
    return out[:rows, :D] + out[:rows, D:] + out[rows:, :D]


def late_rows(x, width):
    return both([x[i : i + width] for i in range(width, ITEMS, 2 * width)], 0)


def drop_late(x, y, width):
    parts = []
    for n, i in enumerate(range(0, ITEMS, 2 * width)):
        parts += [x[i : i + width], x[i + width : i + 2 * width] - y[n * width : (n + 1) * width]]
    return both(parts, 0)


def item_betas(b_rows):
    left = lax.broadcasted_iota(jnp.int32, (1, ITEMS), 1) < HALF
    rows = []
    for h in range(PER):
        pair = [b_rows[pl.ds((pl.program_id(0) * PER + h) * 2 + j, 1), :] for j in range(2)]
        for c in range(BLOCKS // 2):
            lanes = slice(c * ITEMS, (c + 1) * ITEMS)
            first, second = pair[0][:, lanes], pair[1][:, lanes]
            rows.append(jnp.where(left, first, pltpu.roll(second, HALF, 1)))
            rows.append(jnp.where(left, pltpu.roll(first, HALF, 1), second))
    return both(rows, 0)


def local_maps_kernel(k_all, v_all, b_ref, wu_ref, r_ref, tot_ref, k_held, v_held, arrived):
    step_now = pl.program_id(0)

    def fetch(source, held, which, step):
        columns = pl.ds(pl.multiple_of(step * PER * 2 * D, PER * 2 * D), PER * 2 * D)
        return pltpu.make_async_copy(source.at[:, columns], held.at[step], arrived.at[which, step])

    @pl.when(step_now == 0)
    def _():
        for step in range(HEADS // PER):
            fetch(k_all, k_held, 0, step).start()
            fetch(v_all, v_held, 1, step).start()

    fetch(k_all, k_held, 0, step_now).wait()
    k_ref, v_ref = k_held.at[step_now], v_held.at[step_now]
    shape = (ITEMS, ITEMS)
    ni, nj = order(shape, 0), order(shape, 1)
    eye = (ni == nj).astype(F32)
    masks = []
    for level in range(7):
        hit = ((ni >> (level + 1)) == (nj >> (level + 1))) & ((ni >> level) > (nj >> level))
        masks.append(hit.astype(F32))
    low = [m.astype(BF16) for m in masks]
    units = [(h, b) for h in range(PER) for b in range(BLOCKS)]
    keys = [block_keys(k_ref, h, b) for h, b in units]
    grams = [mm_nt(k, k) for k in keys]
    squares = both([jnp.sum(g * eye, 0, keepdims=True) for g in grams], 0)
    pairs = both([jnp.sum(g * masks[0], 0, keepdims=True) for g in grams], 0)
    rk = lax.rsqrt(squares + 1e-06)
    beta_rk = item_betas(b_ref) * rk
    beta_rk2 = beta_rk * rk
    pairs = pairs * pltpu.roll(beta_rk2, HALF, 1)
    columns = beta_rk2.T
    pair_columns = pairs.T
    inv, pieces = [], []
    for i, g in enumerate(grams):
        l = columns[:, i : i + 1] * g
        x = l * masks[1]
        x = both([x[:HALF], x[HALF:] - pair_columns[:HALF, i : i + 1] * x[:HALF]], 0)
        x = x - pltpu.roll(x, HALF, 1) * pairs[i : i + 1]
        inv.append(eye - l * masks[0] - x)
        pieces.append(split(l))
    for level in range(2, 7):
        m = low[level]
        width = 1 << (level - 1)
        cut = [split(t) for t in inv]
        if width >= 8:
            left = [split(late_rows(t, width)) for t in inv] if width < 16 else [(late_rows(c[0], width), late_rows(c[1], width)) for c in cut]
        else:
            left = cut
        prod = stacked3 if width >= 8 else narrow3
        step = [prod(*t, p[0] * m, p[1] * m) for t, p in zip(left, pieces)]
        step = [prod(*split(x), *c) for x, c in zip(step, cut)]
        if width >= 8:
            inv = [drop_late(t, x, width) for t, x in zip(inv, step)]
        else:
            inv = [t - x for t, x in zip(inv, step)]
    maps = []
    fetch(v_all, v_held, 1, step_now).wait()
    for i, (h, b) in enumerate(units):
        v = block_keys(v_ref, h, b)
        w = mm(both(split(inv[i] * beta_rk2[i : i + 1]), 1), both([keys[i], keys[i]], 0))
        u = mm(both(split(inv[i] * beta_rk[i : i + 1]), 1), both([v, v], 0))
        wh, wl = split(w)
        uh, ul = split(u)
        wu = both([wh, uh, wl, ul], 1)
        wu_ref[h, b] = wu
        r = mm_tn(keys[i], wu)
        r = r[:, : 2 * D] + r[:, 2 * D :]
        maps.append(both([eye - r[:, :D], r[:, D:]], 1))

    def keep(h, b, m):
        hi, lo = split(m)
        r_ref[h, b - 1] = both([hi, lo], 1)

    two = [join(maps[i], maps[i + 1]) for i in range(0, len(maps), 2)]
    four = [join(two[i], two[i + 1]) for i in range(0, len(two), 2)]
    for h in range(PER):
        m, t, f = maps[h * 8 :], two[h * 4 :], four[h * 2 :]
        for b, node in ((1, m[0]), (2, t[0]), (3, m[2]), (4, f[0]), (5, m[4]), (6, t[2]), (7, m[6])):
            keep(h, b, node)
        tot_ref[h] = join(f[0], f[1])


def local_maps(keys, values, betas):
    return pl.pallas_call(
        local_maps_kernel,
        grid=(HEADS // PER,),
        in_specs=[
            pl.BlockSpec(memory_space=pltpu.HBM),
            pl.BlockSpec(memory_space=pltpu.HBM),
            pl.BlockSpec((2 * HEADS, BLOCKS * HALF), lambda h: (0, 0)),
        ],
        out_specs=[
            pl.BlockSpec((PER, BLOCKS, ITEMS, 4 * D), lambda h: (h, 0, 0, 0)),
            pl.BlockSpec((PER, BLOCKS - 1, D, 4 * D), lambda h: (h, 0, 0, 0)),
            pl.BlockSpec((PER, D, 2 * D), lambda h: (h, 0, 0)),
        ],
        out_shape=[
            jax.ShapeDtypeStruct((HEADS, BLOCKS, ITEMS, 4 * D), BF16),
            jax.ShapeDtypeStruct((HEADS, BLOCKS - 1, D, 4 * D), BF16),
            jax.ShapeDtypeStruct((HEADS, D, 2 * D), F32),
        ],
        scratch_shapes=[
            pltpu.VMEM((HEADS // PER, BLOCKS * HALF, PER * 2 * D), BF16),
            pltpu.VMEM((HEADS // PER, BLOCKS * HALF, PER * 2 * D), BF16),
            pltpu.SemaphoreType.DMA((2, HEADS // PER)),
        ],
        compiler_params=pltpu.CompilerParams(vmem_limit_bytes=VMEM_LIMIT),
        name="local_maps",
    )(keys, values, betas)


def block_terms(q_ref, k_ref, wu_ref, b):
    shape = (HALF, ITEMS)
    seen = (
        lax.broadcasted_iota(jnp.int32, shape, 1) % HALF <= lax.broadcasted_iota(jnp.int32, shape, 0)
    ).astype(F32)
    q = q_ref[b * HALF : (b + 1) * HALF, :]
    qf = q.astype(F32)
    sh, sl = split(mm_nt(q, block_keys(k_ref, 0, b)) * seen)
    wu = wu_ref[0, b]
    x = wide3(sh, sl, wu[:, : 2 * D], wu[:, 2 * D :])
    rq = lax.rsqrt(jnp.sum(qf * qf, -1, keepdims=True) + 1e-06)
    return (qf - x[:, :D]) * rq, x[:, D:] * rq


def entry_terms(terms, r_ref, qe_ref, ol_ref):
    node = [None] + [(r_ref[0, b][:, : 2 * D], r_ref[0, b][:, 2 * D :]) for b in range(BLOCKS - 1)]

    def onto(early, late):
        out = wide3(late[0][:, :D], late[1][:, :D], *early)
        added = late[0][:, D:].astype(F32) + late[1][:, D:].astype(F32)
        return split(both([out[:, :D], out[:, D:] + added], 1))

    prefix = list(node)
    prefix[3] = onto(node[2], node[3])
    prefix[5] = onto(node[4], node[5])
    prefix[6] = onto(node[4], node[6])
    prefix[7] = onto(prefix[6], node[7])
    for b in range(BLOCKS):
        rows = slice(b * HALF, (b + 1) * HALF)
        qe, ol = terms(b)
        if b:
            x = wide3(*split(qe), *prefix[b])
            qe, ol = x[:, :D], x[:, D:] + ol
        qe_ref[0, rows, :] = qe
        ol_ref[0, rows, :] = ol


def first_terms_kernel(q_ref, k_ref, wu_ref, qe_ref, ol_ref):
    for b in range(BLOCKS):
        rows = slice(b * HALF, (b + 1) * HALF)
        qe_ref[0, rows, :], ol_ref[0, rows, :] = block_terms(q_ref, k_ref, wu_ref, b)


def first_outputs_kernel(qb_ref, ob_ref, r_ref, qe_ref, ol_ref):
    def terms(b):
        rows = slice(b * HALF, (b + 1) * HALF)
        return qb_ref[0, rows, :], ob_ref[0, rows, :]

    entry_terms(terms, r_ref, qe_ref, ol_ref)


def last_outputs_kernel(q_ref, k_ref, wu_ref, r_ref, qe_ref, ol_ref):
    entry_terms(functools.partial(block_terms, q_ref, k_ref, wu_ref), r_ref, qe_ref, ol_ref)


def per_head(kernel, name, arrays, kinds, first, heads, units, limit):
    makers = {
        "q": pl.BlockSpec((BLOCKS * HALF, D), lambda h: (0, h + first)),
        "k": pl.BlockSpec((BLOCKS * HALF, 2 * D), lambda h: (0, h + first)),
        "w": pl.BlockSpec((1, BLOCKS, ITEMS, 4 * D), lambda h: (h + first, 0, 0, 0)),
        "r": pl.BlockSpec((1, BLOCKS - 1, D, 4 * D), lambda h: (h + first, 0, 0, 0)),
        "t": pl.BlockSpec((1, BLOCKS * HALF, D), lambda h: (h, 0, 0)),
    }
    return pl.pallas_call(
        kernel,
        grid=(heads,),
        in_specs=[makers[kind] for kind in kinds],
        out_specs=[makers["t"]] * 2,
        out_shape=[jax.ShapeDtypeStruct((heads, BLOCKS * HALF, D), F32)] * 2,
        compiler_params=pltpu.CompilerParams(vmem_limit_bytes=limit),
        cost_estimate=pl.CostEstimate(
            flops=2 * heads * BLOCKS * HALF * D * D * units, bytes_accessed=6 * 1024 * 1024, transcendentals=0
        ),
        name=name,
    )(*arrays)


def in_vmem(n):
    return [pl.BlockSpec(memory_space=pltpu.VMEM)] * n


def in_smem():
    return [pl.BlockSpec(memory_space=pltpu.SMEM)]


def row_maps_kernel(me_ref, own_ref, r1, r2, r3, pre_ref, tot_ref, held):
    y = me_ref[0]
    held[y] = own_ref[...]
    for s, ref in ((1, r1), (2, r2), (3, r3)):
        held[(y + NY - s) % NY] = ref[...]
    two = join(held[0], held[1])
    pre_ref[0] = held[0]
    pre_ref[1] = two
    pre_ref[2] = join(two, held[2])
    tot_ref[...] = join(two, join(held[2], held[3]))


def plane_maps_kernel(me_ref, own_ref, r1, r2, r3, s0_ref, pre_ref, end_ref, s0t_ref, held):
    y, z = me_ref[0], me_ref[1] % 4
    held[z] = own_ref[...]
    for s, ref in ((1, r1), (2, r2), (3, r3)):
        held[(z + 4 - s) % 4] = ref[...]
    start = s0_ref[y].T
    s0t_ref[...] = start
    two = join(held[0], held[1])
    prefixes = (held[0], two, join(two, held[2]))
    pre_ref[...] = prefixes[0]
    for i in (2, 3):

        @pl.when(z == i)
        def _():
            pre_ref[...] = prefixes[i - 1]

    end_ref[...] = apply(join(held[2], held[3]), apply(two, start))


def apply(m, state):
    return narrow3(*split(m[:, :D]), *split(state)) + m[:, D:]


def states_kernel(me_ref, s0t_ref, mid_ref, pre_ref, rows_ref, out_ref):
    z = me_ref[1]
    base = jnp.where(z >= 4, mid_ref[...], s0t_ref[...])
    state = jnp.where(z % 4 > 0, apply(pre_ref[...], base), base)
    out_ref[0] = state
    for i in range(1, NY):
        out_ref[i] = apply(rows_ref[i - 1], state)


def finish_kernel(me_ref, s0, s1, s2, s3, qa_ref, oa_ref, qb_ref, ob_ref, g_ref, out_ref, held):
    y = me_ref[0]
    for s, ref in enumerate((s0, s1, s2, s3)):
        held[(y + NY - s) % NY] = ref[...]
    for h in range(HEADS):
        qe, ol = (qa_ref[h], oa_ref[h]) if h < EARLY else (qb_ref[h - EARLY], ob_ref[h - EARLY])
        raw = narrow3(*split(qe), *split(held[h])) + ol
        scale = lax.rsqrt(jnp.mean(raw * raw, -1, keepdims=True) + 1e-06)
        out_ref[:, h * D : (h + 1) * D] = (raw * scale * g_ref[h]).astype(BF16)


def call(kernel, n_in, out_shape, scratch=(), name=None):
    return pl.pallas_call(
        kernel,
        in_specs=in_smem() + in_vmem(n_in),
        out_specs=jax.tree.map(lambda _: pl.BlockSpec(memory_space=pltpu.VMEM), out_shape),
        out_shape=out_shape,
        scratch_shapes=list(scratch),
        compiler_params=pltpu.CompilerParams(vmem_limit_bytes=SMALL_LIMIT),
        name=name,
    )


def shift_y(s):
    return [(z * NY + y, z * NY + (y + s) % NY) for z in range(NZ) for y in range(NY)]


def shift_z(s):
    return [
        (z * NY + y, (z // 4 * 4 + (z % 4 + s) % 4) * NY + y) for z in range(NZ) for y in range(NY)
    ]


ACROSS = [(a * NY + y, b * NY + y) for a, b in zip(range(NZ), (7, 6, 5, 4, 3, 2, 1, 0)) for y in range(NY)]


def body(queries, keys, values, betas, initial_state, out_gain):
    f32 = lambda *shape: jax.ShapeDtypeStruct(shape, F32)
    place = lax.axis_index("ctx").astype(jnp.int32)
    y, z = place % NY, place // NY
    me = jnp.stack([y, z])
    wu, prefixes, total = local_maps(keys, values, betas.T)

    def exchange(array):
        mine = [lax.dynamic_index_in_dim(array, (y + s) % NY, 0, False) for s in range(NY)]
        return mine[:1] + [lax.ppermute(mine[s], "ctx", shift_y(s)) for s in (1, 2, 3)]

    arrived = exchange(total)
    terms = per_head(
        first_terms_kernel, "first_terms", (queries, keys, wu), "qkw", 0, EARLY, 7, TERMS_LIMIT
    )
    arrived, terms = lax.optimization_barrier((arrived, terms))
    rows_pre, row_total = call(
        row_maps_kernel, 4, [f32(3, D, 2 * D), f32(D, 2 * D)], [pltpu.VMEM((4, D, 2 * D), F32)], "row_maps"
    )(me, *arrived)
    others = [lax.ppermute(row_total, "ctx", shift_z(s)) for s in (1, 2, 3)]
    first = per_head(
        first_outputs_kernel, "first_outputs", (*terms, prefixes), "ttr", 0, EARLY, 10, OUTPUTS_LIMIT
    )
    last = per_head(
        last_outputs_kernel,
        "last_outputs",
        (queries, keys, wu, prefixes),
        "qkwr",
        EARLY,
        HEADS - EARLY,
        17,
        OUTPUTS_LIMIT,
    )
    others, first, last = lax.optimization_barrier((others, first, last))
    plane_pre, end, start = call(
        plane_maps_kernel,
        5,
        [f32(D, 2 * D), f32(D, D), f32(D, D)],
        [pltpu.VMEM((4, D, 2 * D), F32)],
        "plane_maps",
    )(me, row_total, *others, initial_state)
    mid = lax.ppermute(end, "ctx", ACROSS)
    states = call(states_kernel, 4, f32(NY, D, D), (), "states")(me, start, mid, plane_pre, rows_pre)
    local_out = call(
        finish_kernel,
        9,
        jax.ShapeDtypeStruct((BLOCKS * HALF, HEADS * D), BF16),
        [pltpu.VMEM((NY, D, D), F32)],
        "finish",
    )(me, *exchange(states), *first, *last, out_gain.reshape(HEADS, 1, D))
    return lax.all_to_all(local_out, "head", split_axis=0, concat_axis=1, tiled=True)


def solution(mesh):
    placed = (
        P("ctx", "head"),
        P("ctx", "head"),
        P("ctx", "head"),
        P("ctx", "head"),
        P("head", None, None),
        P("head"),
    )
    return jax.shard_map(
        body, mesh=mesh, in_specs=placed, out_specs=P(("ctx", "head"), None), check_vma=False
    )
```

```python
import functools
import jax
import jax.numpy as jnp
from jax import lax
from jax.experimental import pallas as pl
from jax.experimental.pallas import tpu as pltpu
from jax.sharding import PartitionSpec as P

D = 128
HALF = 64
ITEMS = 128
BLOCKS = 8
HEADS = 4
NY = 4
EARLY = 2
NZ = 8
F32 = jnp.float32
BF16 = jnp.bfloat16
VMEM_LIMIT = 53 * 1024 * 1024
TERMS_LIMIT = 60 * 1024 * 1024
OUTPUTS_LIMIT = 48 * 1024 * 1024
SMALL_LIMIT = 16 * 1024 * 1024
PER = 2


def split(x):
    hi = x.astype(BF16)
    lo = (x - hi.astype(F32)).astype(BF16)
    return hi, lo


def mm(a, b):
    return lax.dot_general(a, b, (((1,), (0,)), ((), ())), preferred_element_type=F32)


def mm_nt(a, b):
    return lax.dot_general(a, b, (((1,), (1,)), ((), ())), preferred_element_type=F32)


def mm_tn(a, b):
    return lax.dot_general(a, b, (((0,), (0,)), ((), ())), preferred_element_type=F32)


def both(parts, axis):
    return jnp.concatenate(parts, axis)


def narrow3(ah, al, bh, bl):
    right = both([bh, bl], 1)
    out = mm(both([ah, al], 1), both([right, right], 0))
    return out[:, :D] + out[:, D:]


def wide3(ah, al, bh, bl):
    return mm(both([ah, al], 1), both([bh, bh], 0)) + mm(ah, bl)


def join(early, late):
    out = wide3(*split(late[:, :D]), *split(early))
    return both([out[:, :D], out[:, D:] + late[:, D:]], 1)


def order(shape, axis):
    place = lax.broadcasted_iota(jnp.int32, shape, axis)
    return 2 * (place % HALF) + place // HALF


def block_keys(ref, h, b):
    rows = slice(b * HALF, (b + 1) * HALF)
    return both([ref[rows, 2 * h * D : (2 * h + 1) * D], ref[rows, (2 * h + 1) * D : (2 * h + 2) * D]], 0)


def stacked3(ah, al, bh, bl):
    rows = ah.shape[0]
    out = mm(both([ah, al], 0), both([bh, bl], 1))
    return out[:rows, :D] + out[:rows, D:] + out[rows:, :D]


def late_rows(x, width):
    return both([x[i : i + width] for i in range(width, ITEMS, 2 * width)], 0)


def drop_late(x, y, width):
    parts = []
    for n, i in enumerate(range(0, ITEMS, 2 * width)):
        parts += [x[i : i + width], x[i + width : i + 2 * width] - y[n * width : (n + 1) * width]]
    return both(parts, 0)


def item_betas(b_rows):
    left = lax.broadcasted_iota(jnp.int32, (1, ITEMS), 1) < HALF
    rows = []
    for h in range(PER):
        pair = [b_rows[pl.ds((pl.program_id(0) * PER + h) * 2 + j, 1), :] for j in range(2)]
        for c in range(BLOCKS // 2):
            lanes = slice(c * ITEMS, (c + 1) * ITEMS)
            first, second = pair[0][:, lanes], pair[1][:, lanes]
            rows.append(jnp.where(left, first, pltpu.roll(second, HALF, 1)))
            rows.append(jnp.where(left, pltpu.roll(first, HALF, 1), second))
    return both(rows, 0)


def local_maps_kernel(k_all, v_all, b_ref, wu_ref, r_ref, tot_ref, k_held, v_held, arrived):
    step_now = pl.program_id(0)

    def fetch(source, held, which, step):
        columns = pl.ds(pl.multiple_of(step * PER * 2 * D, PER * 2 * D), PER * 2 * D)
        return pltpu.make_async_copy(source.at[:, columns], held.at[step], arrived.at[which, step])

    @pl.when(step_now == 0)
    def _():
        for step in range(HEADS // PER):
            fetch(k_all, k_held, 0, step).start()
            fetch(v_all, v_held, 1, step).start()

    fetch(k_all, k_held, 0, step_now).wait()
    k_ref, v_ref = k_held.at[step_now], v_held.at[step_now]
    shape = (ITEMS, ITEMS)
    ni, nj = order(shape, 0), order(shape, 1)
    eye = (ni == nj).astype(F32)
    masks = []
    for level in range(7):
        hit = ((ni >> (level + 1)) == (nj >> (level + 1))) & ((ni >> level) > (nj >> level))
        masks.append(hit.astype(F32))
    low = [m.astype(BF16) for m in masks]
    units = [(h, b) for h in range(PER) for b in range(BLOCKS)]
    keys = [block_keys(k_ref, h, b) for h, b in units]
    grams = [mm_nt(k, k) for k in keys]
    squares = both([jnp.sum(g * eye, 0, keepdims=True) for g in grams], 0)
    pairs = both([jnp.sum(g * masks[0], 0, keepdims=True) for g in grams], 0)
    rk = lax.rsqrt(squares + 1e-06)
    beta_rk = item_betas(b_ref) * rk
    beta_rk2 = beta_rk * rk
    pairs = pairs * pltpu.roll(beta_rk2, HALF, 1)
    columns = beta_rk2.T
    pair_columns = pairs.T
    inv, pieces = [], []
    for i, g in enumerate(grams):
        l = columns[:, i : i + 1] * g
        x = l * masks[1]
        x = both([x[:HALF], x[HALF:] - pair_columns[:HALF, i : i + 1] * x[:HALF]], 0)
        x = x - pltpu.roll(x, HALF, 1) * pairs[i : i + 1]
        inv.append(eye - l * masks[0] - x)
        pieces.append(split(l))
    for level in range(2, 7):
        m = low[level]
        width = 1 << (level - 1)
        cut = [split(t) for t in inv]
        if width >= 8:
            left = [split(late_rows(t, width)) for t in inv] if width < 16 else [(late_rows(c[0], width), late_rows(c[1], width)) for c in cut]
        else:
            left = cut
        prod = stacked3 if width >= 8 else narrow3
        step = [prod(*t, p[0] * m, p[1] * m) for t, p in zip(left, pieces)]
        step = [prod(*split(x), *c) for x, c in zip(step, cut)]
        if width >= 8:
            inv = [drop_late(t, x, width) for t, x in zip(inv, step)]
        else:
            inv = [t - x for t, x in zip(inv, step)]
    maps = []
    fetch(v_all, v_held, 1, step_now).wait()
    for i, (h, b) in enumerate(units):
        v = block_keys(v_ref, h, b)
        w = mm(both(split(inv[i] * beta_rk2[i : i + 1]), 1), both([keys[i], keys[i]], 0))
        u = mm(both(split(inv[i] * beta_rk[i : i + 1]), 1), both([v, v], 0))
        wh, wl = split(w)
        uh, ul = split(u)
        wu = both([wh, uh, wl, ul], 1)
        wu_ref[h, b] = wu
        r = mm_tn(keys[i], wu)
        r = r[:, : 2 * D] + r[:, 2 * D :]
        maps.append(both([eye - r[:, :D], r[:, D:]], 1))

    def keep(h, b, m):
        hi, lo = split(m)
        r_ref[h, b - 1] = both([hi, lo], 1)

    two = [join(maps[i], maps[i + 1]) for i in range(0, len(maps), 2)]
    four = [join(two[i], two[i + 1]) for i in range(0, len(two), 2)]
    for h in range(PER):
        m, t, f = maps[h * 8 :], two[h * 4 :], four[h * 2 :]
        for b, node in ((1, m[0]), (2, t[0]), (3, m[2]), (4, f[0]), (5, m[4]), (6, t[2]), (7, m[6])):
            keep(h, b, node)
        tot_ref[h] = join(f[0], f[1])


def local_maps(keys, values, betas):
    return pl.pallas_call(
        local_maps_kernel,
        grid=(HEADS // PER,),
        in_specs=[
            pl.BlockSpec(memory_space=pltpu.HBM),
            pl.BlockSpec(memory_space=pltpu.HBM),
            pl.BlockSpec((2 * HEADS, BLOCKS * HALF), lambda h: (0, 0)),
        ],
        out_specs=[
            pl.BlockSpec((PER, BLOCKS, ITEMS, 4 * D), lambda h: (h, 0, 0, 0)),
            pl.BlockSpec((PER, BLOCKS - 1, D, 4 * D), lambda h: (h, 0, 0, 0)),
            pl.BlockSpec((PER, D, 2 * D), lambda h: (h, 0, 0)),
        ],
        out_shape=[
            jax.ShapeDtypeStruct((HEADS, BLOCKS, ITEMS, 4 * D), BF16),
            jax.ShapeDtypeStruct((HEADS, BLOCKS - 1, D, 4 * D), BF16),
            jax.ShapeDtypeStruct((HEADS, D, 2 * D), F32),
        ],
        scratch_shapes=[
            pltpu.VMEM((HEADS // PER, BLOCKS * HALF, PER * 2 * D), BF16),
            pltpu.VMEM((HEADS // PER, BLOCKS * HALF, PER * 2 * D), BF16),
            pltpu.SemaphoreType.DMA((2, HEADS // PER)),
        ],
        compiler_params=pltpu.CompilerParams(vmem_limit_bytes=VMEM_LIMIT),
        name="local_maps",
    )(keys, values, betas)


def block_terms(q_ref, k_ref, wu_ref, b):
    shape = (HALF, ITEMS)
    seen = (
        lax.broadcasted_iota(jnp.int32, shape, 1) % HALF <= lax.broadcasted_iota(jnp.int32, shape, 0)
    ).astype(F32)
    q = q_ref[b * HALF : (b + 1) * HALF, :]
    qf = q.astype(F32)
    sh, sl = split(mm_nt(q, block_keys(k_ref, 0, b)) * seen)
    wu = wu_ref[0, b]
    x = wide3(sh, sl, wu[:, : 2 * D], wu[:, 2 * D :])
    rq = lax.rsqrt(jnp.sum(qf * qf, -1, keepdims=True) + 1e-06)
    return (qf - x[:, :D]) * rq, x[:, D:] * rq


def entry_terms(terms, r_ref, qe_ref, ol_ref):
    node = [None] + [(r_ref[0, b][:, : 2 * D], r_ref[0, b][:, 2 * D :]) for b in range(BLOCKS - 1)]

    def onto(early, late):
        out = wide3(late[0][:, :D], late[1][:, :D], *early)
        added = late[0][:, D:].astype(F32) + late[1][:, D:].astype(F32)
        return split(both([out[:, :D], out[:, D:] + added], 1))

    prefix = list(node)
    prefix[3] = onto(node[2], node[3])
    prefix[5] = onto(node[4], node[5])
    prefix[6] = onto(node[4], node[6])
    prefix[7] = onto(prefix[6], node[7])
    for b in range(BLOCKS):
        rows = slice(b * HALF, (b + 1) * HALF)
        qe, ol = terms(b)
        if b:
            x = wide3(*split(qe), *prefix[b])
            qe, ol = x[:, :D], x[:, D:] + ol
        qe_ref[0, rows, :] = qe
        ol_ref[0, rows, :] = ol


def first_terms_kernel(q_ref, k_ref, wu_ref, qe_ref, ol_ref):
    for b in range(BLOCKS):
        rows = slice(b * HALF, (b + 1) * HALF)
        qe_ref[0, rows, :], ol_ref[0, rows, :] = block_terms(q_ref, k_ref, wu_ref, b)


def first_outputs_kernel(qb_ref, ob_ref, r_ref, qe_ref, ol_ref):
    def terms(b):
        rows = slice(b * HALF, (b + 1) * HALF)
        return qb_ref[0, rows, :], ob_ref[0, rows, :]

    entry_terms(terms, r_ref, qe_ref, ol_ref)


def last_outputs_kernel(q_ref, k_ref, wu_ref, r_ref, qe_ref, ol_ref):
    entry_terms(functools.partial(block_terms, q_ref, k_ref, wu_ref), r_ref, qe_ref, ol_ref)


def per_head(kernel, name, arrays, kinds, first, heads, units, limit):
    makers = {
        "q": pl.BlockSpec((BLOCKS * HALF, D), lambda h: (0, h + first)),
        "k": pl.BlockSpec((BLOCKS * HALF, 2 * D), lambda h: (0, h + first)),
        "w": pl.BlockSpec((1, BLOCKS, ITEMS, 4 * D), lambda h: (h + first, 0, 0, 0)),
        "r": pl.BlockSpec((1, BLOCKS - 1, D, 4 * D), lambda h: (h + first, 0, 0, 0)),
        "t": pl.BlockSpec((1, BLOCKS * HALF, D), lambda h: (h, 0, 0)),
    }
    return pl.pallas_call(
        kernel,
        grid=(heads,),
        in_specs=[makers[kind] for kind in kinds],
        out_specs=[makers["t"]] * 2,
        out_shape=[jax.ShapeDtypeStruct((heads, BLOCKS * HALF, D), F32)] * 2,
        compiler_params=pltpu.CompilerParams(vmem_limit_bytes=limit),
        cost_estimate=pl.CostEstimate(
            flops=2 * heads * BLOCKS * HALF * D * D * units, bytes_accessed=6 * 1024 * 1024, transcendentals=0
        ),
        name=name,
    )(*arrays)


def in_vmem(n):
    return [pl.BlockSpec(memory_space=pltpu.VMEM)] * n


def in_smem():
    return [pl.BlockSpec(memory_space=pltpu.SMEM)]


def row_maps_kernel(me_ref, own_ref, r1, r2, r3, pre_ref, tot_ref, held):
    y = me_ref[0]
    held[y] = own_ref[...]
    for s, ref in ((1, r1), (2, r2), (3, r3)):
        held[(y + NY - s) % NY] = ref[...]
    two = join(held[0], held[1])
    pre_ref[0] = held[0]
    pre_ref[1] = two
    pre_ref[2] = join(two, held[2])
    tot_ref[...] = join(two, join(held[2], held[3]))


def plane_maps_kernel(me_ref, own_ref, r1, r2, r3, s0_ref, pre_ref, end_ref, s0t_ref, held):
    y, z = me_ref[0], me_ref[1] % 4
    held[z] = own_ref[...]
    for s, ref in ((1, r1), (2, r2), (3, r3)):
        held[(z + 4 - s) % 4] = ref[...]
    start = s0_ref[y].T
    s0t_ref[...] = start
    two = join(held[0], held[1])
    prefixes = (held[0], two, join(two, held[2]))
    pre_ref[...] = prefixes[0]
    for i in (2, 3):

        @pl.when(z == i)
        def _():
            pre_ref[...] = prefixes[i - 1]

    end_ref[...] = apply(join(held[2], held[3]), apply(two, start))


def apply(m, state):
    return narrow3(*split(m[:, :D]), *split(state)) + m[:, D:]


def state_maps_kernel(me_ref, pre_ref, rows_ref, maps_ref):
    inner = me_ref[1] % 4 > 0
    pre = pre_ref[...]
    i = lax.broadcasted_iota(jnp.int32, (D, 2 * D), 0)
    j = lax.broadcasted_iota(jnp.int32, (D, 2 * D), 1)
    maps_ref[0] = jnp.where(inner, pre, (i == j).astype(F32))
    for i in range(1, NY):
        late = rows_ref[i - 1]
        maps_ref[i] = jnp.where(inner, join(pre, late), late)


def states_kernel(me_ref, s0t_ref, mid_ref, maps_ref, out_ref):
    base = jnp.where(me_ref[1] >= 4, mid_ref[...], s0t_ref[...])
    for i in range(NY):
        out_ref[i] = apply(maps_ref[i], base)


def finish_kernel(me_ref, s0, s1, s2, s3, qa_ref, oa_ref, qb_ref, ob_ref, g_ref, out_ref, held):
    y = me_ref[0]
    for s, ref in enumerate((s0, s1, s2, s3)):
        held[(y + NY - s) % NY] = ref[...]
    for h in range(HEADS):
        qe, ol = (qa_ref[h], oa_ref[h]) if h < EARLY else (qb_ref[h - EARLY], ob_ref[h - EARLY])
        raw = narrow3(*split(qe), *split(held[h])) + ol
        scale = lax.rsqrt(jnp.mean(raw * raw, -1, keepdims=True) + 1e-06)
        out_ref[:, h * D : (h + 1) * D] = (raw * scale * g_ref[h]).astype(BF16)


def call(kernel, n_in, out_shape, scratch=(), name=None):
    return pl.pallas_call(
        kernel,
        in_specs=in_smem() + in_vmem(n_in),
        out_specs=jax.tree.map(lambda _: pl.BlockSpec(memory_space=pltpu.VMEM), out_shape),
        out_shape=out_shape,
        scratch_shapes=list(scratch),
        compiler_params=pltpu.CompilerParams(vmem_limit_bytes=SMALL_LIMIT),
        name=name,
    )


def shift_y(s):
    return [(z * NY + y, z * NY + (y + s) % NY) for z in range(NZ) for y in range(NY)]


def shift_z(s):
    return [
        (z * NY + y, (z // 4 * 4 + (z % 4 + s) % 4) * NY + y) for z in range(NZ) for y in range(NY)
    ]


ACROSS = [(a * NY + y, b * NY + y) for a, b in zip(range(NZ), (7, 6, 5, 4, 3, 2, 1, 0)) for y in range(NY)]


def body(queries, keys, values, betas, initial_state, out_gain):
    f32 = lambda *shape: jax.ShapeDtypeStruct(shape, F32)
    place = lax.axis_index("ctx").astype(jnp.int32)
    y, z = place % NY, place // NY
    me = jnp.stack([y, z])
    wu, prefixes, total = local_maps(keys, values, betas.T)

    def exchange(array):
        mine = [lax.dynamic_index_in_dim(array, (y + s) % NY, 0, False) for s in range(NY)]
        return mine[:1] + [lax.ppermute(mine[s], "ctx", shift_y(s)) for s in (1, 2, 3)]

    arrived = exchange(total)
    terms = per_head(
        first_terms_kernel, "first_terms", (queries, keys, wu), "qkw", 0, EARLY, 7, TERMS_LIMIT
    )
    arrived, terms = lax.optimization_barrier((arrived, terms))
    rows_pre, row_total = call(
        row_maps_kernel, 4, [f32(3, D, 2 * D), f32(D, 2 * D)], [pltpu.VMEM((4, D, 2 * D), F32)], "row_maps"
    )(me, *arrived)
    others = [lax.ppermute(row_total, "ctx", shift_z(s)) for s in (1, 2, 3)]
    first = per_head(
        first_outputs_kernel, "first_outputs", (*terms, prefixes), "ttr", 0, EARLY, 10, OUTPUTS_LIMIT
    )
    last = per_head(
        last_outputs_kernel,
        "last_outputs",
        (queries, keys, wu, prefixes),
        "qkwr",
        EARLY,
        HEADS - EARLY,
        17,
        OUTPUTS_LIMIT,
    )
    others, first, last = lax.optimization_barrier((others, first, last))
    plane_pre, end, start = call(
        plane_maps_kernel,
        5,
        [f32(D, 2 * D), f32(D, D), f32(D, D)],
        [pltpu.VMEM((4, D, 2 * D), F32)],
        "plane_maps",
    )(me, row_total, *others, initial_state)
    mid = lax.ppermute(end, "ctx", ACROSS)
    maps = call(state_maps_kernel, 2, f32(NY, D, 2 * D), (), "state_maps")(me, plane_pre, rows_pre)
    mid, maps = lax.optimization_barrier((mid, maps))
    states = call(states_kernel, 3, f32(NY, D, D), (), "states")(me, start, mid, maps)
    local_out = call(
        finish_kernel,
        9,
        jax.ShapeDtypeStruct((BLOCKS * HALF, HEADS * D), BF16),
        [pltpu.VMEM((NY, D, D), F32)],
        "finish",
    )(me, *exchange(states), *first, *last, out_gain.reshape(HEADS, 1, D))
    return lax.all_to_all(local_out, "head", split_axis=0, concat_axis=1, tiled=True)


def solution(mesh):
    placed = (
        P("ctx", "head"),
        P("ctx", "head"),
        P("ctx", "head"),
        P("ctx", "head"),
        P("head", None, None),
        P("head"),
    )
    return jax.shard_map(
        body, mesh=mesh, in_specs=placed, out_specs=P(("ctx", "head"), None), check_vma=False
    )
```
